512 devices in a mesh: row: 32 (over y, x, core), col: 16 (over z).
Axes of the slice: x: 4, y: 4, z: 16, core: 2. Of those that a mesh axis runs over, the one named last changes fastest.
Arguments:
- matrix: float32 [2, 32, 4, 16, 256, 256], P(None, 'row', None, 'col'), may hold values from -8 to 392, as said below
- structure: int32 [2, 64], replicated, may hold values from 0 to 1, as said below
Outputs:
- factored: float32 [2, 32, 4, 16, 256, 256], P(None, 'row', None, 'col')
The draws below stay inside these ranges and needn't reach their ends.
Inputs may be any that keep to these rules, and one draw needn't show every extreme that they name: matrix: each diagonal block has roughly 6 * sqrt(256) times its row and column scale on its diagonal, so every diagonal block met in the reference program is positive definite; the diagonal entries are the largest values. structure[k, i] = 0 for i <= k; structure[0, 1] = 1; structure[1, i] >= structure[0, i] for i >= 2.
All inputs are finite; a program needn't handle non-finite values.
Results may differ from the reference program's by a relative error of at most 0.0001.
Values sent between devices are 32-bit elements; how exact they have to be, the bound alone decides.
No kernel may reach another device: no remote copies, remote signals or barrier semaphores. Data moves between devices by JAX's collectives and lax.ppermute only.
A program may use at most 64 MiB of HBM per device.

```python
import math
import jax
import jax.numpy as jnp
from jax import lax

B = 256
LBR = 2
SUPERNODES = 2
LBC = 4
N_ROW = 32
N_COL = 16


def draw_matrix(key, part):
    key = jax.random.fold_in(key, 11)
    first_key = jax.random.fold_in(key, 0)
    shape = (LBR, N_ROW, LBC, N_COL, B, B)
    grow = (lax.broadcasted_iota(jnp.int32, shape, 0) * N_ROW + lax.broadcasted_iota(jnp.int32, shape, 1)) * B + lax.broadcasted_iota(jnp.int32, shape, 4)
    gcol = (lax.broadcasted_iota(jnp.int32, shape, 2) * N_COL + lax.broadcasted_iota(jnp.int32, shape, 3)) * B + lax.broadcasted_iota(jnp.int32, shape, 5)
    ident = (grow == gcol).astype(jnp.float32)
    base = 6.0 * math.sqrt(B)
    noise = jax.random.truncated_normal(first_key, -6.0, 6.0, shape, jnp.float32)
    values = noise + base * ident
    return values.astype(jnp.float32)


def draw_structure(key, part):
    key = jax.random.fold_in(key, 23)
    first_key, second_key = jax.random.split(key)
    nblocks = LBR * N_ROW
    ids = jnp.arange(nblocks, dtype=jnp.int32)
    first = (jax.random.randint(first_key, (nblocks,), 0, 8) < 4).astype(jnp.int32)
    extra = (jax.random.randint(second_key, (nblocks,), 0, 8) < 3).astype(jnp.int32)
    first = jnp.where(ids == 1, 1, jnp.where(ids > 0, first, 0))
    second = jnp.where(ids > 1, jnp.maximum(first, extra), 0)
    return jnp.stack([first, second]).astype(jnp.int32)


def setup_inputs(seed: int = 0) -> dict:
    key_of = jax.random.split(jax.random.key(seed), 3)
    return {
        "matrix": draw_matrix(jax.random.fold_in(key_of[2], 71), 0),
        "structure": draw_structure(jax.random.fold_in(key_of[2], 71), 0),
    }


def reference(matrix, structure):
    nblocks = LBR * N_ROW
    full = matrix.reshape(nblocks, nblocks, B, B)
    ids = jnp.arange(nblocks, dtype=jnp.int32)
    lower = (ids[:, None] >= ids[None, :]).astype(jnp.float32)
    for step in range(SUPERNODES):
        diag = full[step, step]
        sym = jnp.tril(diag) + jnp.tril(diag, -1).T
        factor = jnp.linalg.cholesky(sym)
        stack = full[:, step].reshape(nblocks * B, B)
        solved = lax.linalg.triangular_solve(factor, stack, left_side=False, lower=True, transpose_a=True)
        solved = solved.reshape(nblocks, B, B)
        keep = structure[step].astype(jnp.float32)
        panel = solved * keep[:, None, None]
        column = jnp.where((ids == step)[:, None, None], jnp.tril(factor)[None], jnp.where((ids > step)[:, None, None], panel, full[:, step]))
        update = jnp.einsum('ias,jbs->ijab', panel, panel, precision=lax.Precision.HIGHEST)
        full = full - lower[:, :, None, None] * update
        full = full.at[:, step].set(column)
    return full.reshape(matrix.shape)
```

```python
import jax
import jax.numpy as jnp
from jax import lax
from jax.experimental import pallas as pl
from jax.experimental.pallas import tpu as pltpu
from jax.sharding import PartitionSpec as P

HIGHEST = lax.Precision.HIGHEST
NX, NY = 4, 4


def row_of(x, y, core):
    return (y % NY) * 2 * NX + (x % NX) * 2 + core


def place_of(row):
    return (row // 2) % NX, row // (2 * NX), row % 2


def plane_shift(dx, dy):
    pairs = []
    for row in range(2 * NX * NY):
        x, y, core = place_of(row)
        pairs.append((row, row_of(x + dx, y + dy, core)))
    return pairs


def mm_t(a, b):
    return lax.dot_general(a, b, (((1,), (1,)), ((), ())), precision=HIGHEST,
                           preferred_element_type=jnp.float32)


def factor_both(a00, a10, a11, keep):
    eye = jnp.eye(a00.shape[0], dtype=jnp.float32)

    def one(block):
        sym = jnp.tril(block) + jnp.tril(block, -1).T
        low = jnp.linalg.cholesky(sym)
        inv = lax.linalg.triangular_solve(low, eye, left_side=True, lower=True)
        return low, inv

    low0, inv0 = one(a00)
    p10 = mm_t(a10, inv0) * keep
    low1, inv1 = one(a11 - mm_t(p10, p10))
    return jnp.concatenate([inv0, p10, inv1]), low0, low1


def spread_diagonal(stacked, col_id):
    nrow = lax.axis_size("row")
    total, width = stacked.shape
    part = lax.all_to_all(stacked.reshape(nrow, total // nrow, width), "row", 0, 0)[0]
    part = jnp.where(col_id == 0, part, 0.0)
    for sources, steps in (((0,), (4, 12, 8)), ((0, 4, 8, 12), (1, 15, 2))):
        sent = [lax.ppermute(part, "col", [(s, (s + d) % 16) for s in sources]) for d in steps]
        part = part + sent[0] + sent[1] + sent[2]
    part = lax.all_to_all(jnp.broadcast_to(part[None], (nrow,) + part.shape), "row", 0, 0)
    return part.reshape(total, width)


def spread_rows(mine, col_id, ncol):
    far = lax.ppermute(mine, "col", [(0, 8), (1, 9)])
    have = jnp.where(col_id < 2, mine, far)
    for step in (4, 2):
        sources = [s for s in range(ncol) if s % (2 * step) < 2]
        up = lax.ppermute(have[0], "col", [(s, (s + step) % ncol) for s in sources])
        down = lax.ppermute(have[1], "col", [(s, (s - step) % ncol) for s in sources])
        have = jnp.where(lax.rem(col_id, 2 * step) < 2, have, jnp.stack([up, down]))
    up = lax.ppermute(have[0], "col", [(s, (s + 1) % ncol) for s in range(ncol)])
    down = lax.ppermute(have[1], "col", [(s, (s - 1) % ncol) for s in range(ncol)])
    near = jnp.stack([up, down])
    even = lax.rem(col_id, 2) == 0
    return jnp.where(even, have, near), jnp.where(even, near, have)


def spread_columns(mine, row_id, nrow, ncol):
    width = mine.shape[-1]
    xpos, ypos, core = place_of(row_id)
    quarter = width // 4
    part = 0.0
    for k in range(4):
        pairs = []
        for row in range(nrow):
            for column in (0, 1):
                target = row_of(k, column + 2 * (row // ncol), 0)
                pairs.append((row * ncol + column, target * ncol + row % ncol))
        part = part + lax.ppermute(mine[:, k * quarter:(k + 1) * quarter], ("row", "col"), pairs)
    swap = [(row, row ^ 1) for row in range(nrow)]
    piece = jnp.where(core == 0, part[0], lax.ppermute(part[1], "row", swap))
    line = jnp.zeros((4, quarter, width), jnp.float32)
    line = lax.dynamic_update_slice(line, piece[None], (xpos, 0, 0))
    for d in (1, 3, 2):
        got = lax.ppermute(piece, "row", plane_shift(d, 0))
        line = lax.dynamic_update_slice(line, got[None], (lax.rem(xpos - d + 4, 4), 0, 0))
    block = line.reshape(width, width)
    got = {d: lax.ppermute(block, "row", plane_shift(0, d)) for d in (1, 3, 2)}
    own = jnp.stack([block, got[1], got[2], got[3]])
    return own, lax.ppermute(own, "row", swap)


def tail_kernel(ids, struct, diag, low0, low1, rows0, rows1, own, other, mat, out, prow, pcol):
    row, col, ypos, core = ids[0], ids[1], ids[2], ids[3]
    width = mat.shape[-1]
    inv0 = diag[0:width, :]
    p10 = diag[width:2 * width, :]
    inv1 = diag[2 * width:3 * width, :]

    def solve(a0, a1, glob):
        keep0 = struct[0, glob].astype(jnp.float32)
        keep1 = struct[1, glob].astype(jnp.float32)
        p0 = mm_t(a0, inv0) * keep0
        p1 = mm_t(a1 - mm_t(p0, p10), inv1) * keep1
        return p0, p1

    for p in range(2):
        p0, p1 = solve(rows0[p], rows1[p], p * 32 + row)
        prow[p, 0] = p0
        prow[p, 1] = p1
    for q in range(4):
        half, high = q % 2, q // 2
        slot0 = lax.rem(ypos - 2 * half + 4, 4)
        slot1 = lax.rem(ypos - 2 * half + 3, 4)
        is_own = core == high
        a0 = jnp.where(is_own, own[slot0], other[slot0])
        a1 = jnp.where(is_own, own[slot1], other[slot1])
        p0, p1 = solve(a0, a1, q * 16 + col)
        pcol[q, 0] = p0
        pcol[q, 1] = p1
    for p in range(2):
        for q in range(4):
            i = p * 32 + row
            j = q * 16 + col
            out[p, q] = mat[p, q]

            @pl.when(i >= j)
            def _():
                out[p, q] = (mat[p, q] - mm_t(prow[p, 0], pcol[q, 0])) - mm_t(prow[p, 1], pcol[q, 1])

            if q == 0:
                @pl.when((j == 0) & (i > 0))
                def _():
                    out[p, q] = prow[p, 0]

                @pl.when((j == 1) & (i > 1))
                def _():
                    out[p, q] = prow[p, 1]

            if p == 0 and q == 0:
                @pl.when((j == 0) & (i == 0))
                def _():
                    out[p, q] = low0[...]

                @pl.when((j == 1) & (i == 1))
                def _():
                    out[p, q] = low1[...]


def on_device(matrix, structure):
    lbr = matrix.shape[0]
    lbc = matrix.shape[2]
    width = matrix.shape[4]
    blocks = matrix.reshape(lbr, lbc, width, width)
    nrow = lax.axis_size("row")
    ncol = lax.axis_size("col")
    row_id = lax.axis_index("row")
    col_id = lax.axis_index("col")
    both = ("row", "col")
    mine = blocks[:, 0]

    a10 = lax.ppermute(mine[0], both, [(ncol, 0)])
    a11 = lax.ppermute(mine[0], both, [(ncol + 1, 0)])
    own, other = spread_columns(mine, row_id, nrow, ncol)
    rows0, rows1 = spread_rows(mine, col_id, ncol)

    block = jax.ShapeDtypeStruct((width, width), jnp.float32)
    stacked, low0, low1 = lax.cond(
        (row_id == 0) & (col_id == 0),
        lambda: factor_both(mine[0], a10, a11, structure[0, 1].astype(jnp.float32)),
        lambda: (jnp.zeros((3 * width, width), jnp.float32),) + (jnp.zeros(block.shape, jnp.float32),) * 2,
    )
    low1 = lax.ppermute(low1, both, [(0, ncol + 1)])
    diag = spread_diagonal(stacked, col_id)

    _, ypos, core = place_of(row_id)
    ids = jnp.stack([row_id, col_id, ypos, core]).astype(jnp.int32)
    vmem = pl.BlockSpec(memory_space=pltpu.VMEM)
    smem = pl.BlockSpec(memory_space=pltpu.SMEM)
    result = pl.pallas_call(
        tail_kernel,
        out_shape=jax.ShapeDtypeStruct(blocks.shape, jnp.float32),
        in_specs=[smem] * 2 + [vmem] * 8,
        out_specs=vmem,
        scratch_shapes=[
            pltpu.VMEM((2, 2, width, width), jnp.float32),
            pltpu.VMEM((4, 2, width, width), jnp.float32),
        ],
        compiler_params=pltpu.CompilerParams(vmem_limit_bytes=40 * 2**20),
    )(ids, structure, diag, low0, low1, rows0, rows1, own, other, blocks)
    return result.reshape(matrix.shape)


def solution(mesh):
    in_specs = (P(None, "row", None, "col", None, None), P())
    out_specs = P(None, "row", None, "col", None, None)
    return jax.shard_map(
        on_device, mesh=mesh, in_specs=in_specs, out_specs=out_specs, check_vma=False
    )
```

```python
import jax
import jax.numpy as jnp
from jax import lax
from jax.experimental import pallas as pl
from jax.experimental.pallas import tpu as pltpu
from jax.sharding import PartitionSpec as P

ROWS = ((1,), (0,))
BOTH = ((1,), (1,))
NX, NY = 4, 4


def row_of(x, y, core):
    return (y % NY) * 2 * NX + (x % NX) * 2 + core


def parts(a):
    high = a.astype(jnp.bfloat16)
    return high, (a - high.astype(jnp.float32)).astype(jnp.bfloat16)


def mul_parts(a, b, dims):
    def one(x, y):
        return lax.dot_general(x, y, (dims, ((), ())), preferred_element_type=jnp.float32)

    return one(a[0], b[0]) + (one(a[0], b[1]) + one(a[1], b[0]))


def mul(a, b, dims):
    return mul_parts(parts(a), parts(b), dims)


def iotas(n):
    return lax.broadcasted_iota(jnp.int32, (n, n), 0), lax.broadcasted_iota(jnp.int32, (n, n), 1)


def inverse_factor(sym, inv):
    n = sym.shape[0]
    ri, ci = iotas(n)
    eye = jnp.where(ri == ci, 1.0, 0.0)
    half = jnp.where(ri > ci, 1.0, jnp.where(ri == ci, 0.5, 0.0))
    diag = jnp.where(ri == ci, sym, 0.0)
    scale_col = lax.rsqrt(jnp.sum(diag, axis=1, keepdims=True))
    scale_row = lax.rsqrt(jnp.sum(diag, axis=0, keepdims=True))
    unit = sym * scale_col * scale_row

    def residual(t):
        return mul(mul(t, unit, ROWS), t, BOTH) - eye

    def improve(carry):
        t, err, _, count = carry
        x = err * half
        t = mul((eye - x) + mul(x, x, ROWS), t, ROWS)
        err = residual(t)
        return t, err, jnp.sum(err * err), count + 1

    x = (unit - eye) * half
    t = (eye - x) + mul(x, x, ROWS)
    err = residual(t)
    start = (t, err, jnp.sum(err * err), jnp.int32(0))
    t, err, size, _ = lax.while_loop(lambda c: (c[2] > 1e-4) & (c[3] < 8), improve, start)
    x = err * half
    near = parts(x)
    x = x - mul_parts(near, near, BOTH) * half
    t = mul((eye - x) + mul_parts(near, near, ROWS), t, ROWS)
    inv[...] = t * scale_row

    @pl.when(jnp.logical_not(size <= 1e-4))
    def _():
        def pivot(k, carry):
            left, right = carry
            row_left = jnp.sum(jnp.where(ri == k, left, 0.0), axis=0, keepdims=True)
            row_right = jnp.sum(jnp.where(ri == k, right, 0.0), axis=0, keepdims=True)
            col = jnp.sum(jnp.where((ci == k) & (ri > k), left, 0.0), axis=1, keepdims=True)
            pick = lax.broadcasted_iota(jnp.int32, (1, n), 1) == k
            col = col / jnp.sum(jnp.where(pick, row_left, 0.0), axis=1, keepdims=True)
            return left - col * row_left, right - col * row_right

        left, right = lax.fori_loop(0, n, pivot, (sym, eye))
        pivots = jnp.sum(jnp.where(ri == ci, left, 0.0), axis=1, keepdims=True)
        inv[...] = right * lax.rsqrt(pivots)


def symmetric(block):
    ri, ci = iotas(block.shape[0])
    return jnp.where(ri >= ci, block, block.T)


def solve(a0, a1, keep0, keep1, inv0, p10, inv1):
    p0 = mul_parts(parts(a0), inv0, BOTH) * keep0
    rest = a1 - mul_parts(parts(p0), p10, BOTH)
    return p0, mul_parts(parts(rest), inv1, BOTH) * keep1


def head_kernel(ids, struct, raw, own, other, inv, low, high, rest, tmp):
    row, col, core = ids[0], ids[1], ids[3]
    n = raw.shape[-1]
    ri, ci = iotas(n)
    s0 = symmetric(raw[:, 0:8, :].reshape(n, n))
    inverse_factor(s0, tmp)
    t0 = tmp[...]
    inv0 = parts(t0)
    a10 = raw[:, 8:16, :].reshape(n, n)
    p10 = mul_parts(parts(a10), inv0, BOTH) * struct[0, 1].astype(jnp.float32)
    half10 = parts(p10)
    s1 = symmetric(raw[:, 16:24, :].reshape(n, n) - mul_parts(half10, half10, BOTH))
    inverse_factor(s1, tmp)
    inv1 = parts(tmp[...])
    for k, pair in enumerate((inv0, half10, inv1)):
        inv[k, 0] = pair[0]
        inv[k, 1] = pair[1]

    @pl.when((row == 0) & (col == 0))
    def _():
        low[...] = jnp.where(ri >= ci, mul_parts(parts(s0), inv0, BOTH), 0.0)

    @pl.when((row == 1) & (col == 1))
    def _():
        low[...] = jnp.where(ri >= ci, mul_parts(parts(s1), inv1, BOTH), 0.0)

    for q in range(4):
        mine = core == q // 2
        slot = 2 * (q % 2)
        a0 = jnp.where(mine, own[slot], other[slot])
        a1 = jnp.where(mine, own[slot + 1], other[slot + 1])
        glob = q * 16 + col
        keep0 = struct[0, glob].astype(jnp.float32)
        keep1 = struct[1, glob].astype(jnp.float32)
        both = solve(a0, a1, keep0, keep1, inv0, half10, inv1)
        for k in range(2):
            top, bottom = parts(both[k])
            high[q, :, k * n:(k + 1) * n] = top
            rest[q, :, k * n:(k + 1) * n] = bottom


def tail_kernel(ids, struct, inv, low, high, rest, rows0, rows1, mat, out, row_high, row_rest):
    row, col = ids[0], ids[1]
    n = mat.shape[-1]
    inv0, p10, inv1 = ((inv[k, 0], inv[k, 1]) for k in range(3))
    for p in range(2):
        i = p * 32 + row
        keep0 = struct[0, i].astype(jnp.float32)
        keep1 = struct[1, i].astype(jnp.float32)
        both = solve(rows0[p], rows1[p], keep0, keep1, inv0, p10, inv1)
        for k in range(2):
            top, bottom = parts(both[k])
            row_high[:, k * n:(k + 1) * n] = top
            row_rest[:, k * n:(k + 1) * n] = bottom
        for q in range(4):
            j = q * 16 + col

            @pl.when(i < j)
            def _():
                out[p, q] = mat[p, q]

            @pl.when(i >= j)
            def _():
                left = (row_high[...], row_rest[...])
                out[p, q] = mat[p, q] - mul_parts(left, (high[q], rest[q]), BOTH)

        @pl.when((col == 0) & (i > 0))
        def _():
            out[p, 0] = both[0]

        @pl.when((col == 1) & (i > 1))
        def _():
            out[p, 0] = both[1]

        if p == 0:
            @pl.when((col < 2) & (row == col))
            def _():
                out[p, 0] = low[...]


def spread_diagonal(first, col_id):
    nrow = lax.axis_size("row")
    ncol = lax.axis_size("col")
    width = first.shape[-1]
    part = lax.all_to_all(first.reshape(nrow, width // nrow, width), "row", 0, 0)[0:2]
    got = [lax.ppermute(part, "col", [(s, s + d) for s in (0, 1)]) for d in (4, 12, 8)]
    part = jnp.where(col_id < 2, part, got[0] + got[1] + got[2])
    sources = [s for s in range(ncol) if s % 4 < 2]
    two_up = lax.ppermute(part, "col", [(s, s + 2) for s in sources])
    mixed = lax.ppermute(part, "col", [(s, (s - 1) % ncol if s % 4 == 0 else s + 1) for s in sources])
    one_up = lax.ppermute(part, "col", [(s, s + 1) for s in sources if s % 4 == 0])
    one_down = lax.ppermute(part[1], "col", [(s, s - 1) for s in sources if s % 4 == 1])
    place = lax.rem(col_id, 4)
    left = jnp.where(place == 0, part, jnp.where(place == 1, one_up, jnp.where(place == 2, two_up, mixed)))
    right = jnp.where(place == 0, one_down, jnp.where(place == 1, part[1], jnp.where(place == 2, mixed[1], two_up[1])))
    part = jnp.concatenate([left[0], left[1], right])
    return lax.all_to_all(jnp.broadcast_to(part[None], (nrow,) + part.shape), "row", 0, 0)


def spread_rows(mine, col_id, ncol):
    far = lax.ppermute(mine, "col", [(0, 8), (1, 9)])
    have = jnp.where(col_id < 2, mine, far)
    for step in (4, 2):
        sources = [s for s in range(ncol) if s % (2 * step) < 2]
        up = lax.ppermute(have[0], "col", [(s, (s + step) % ncol) for s in sources])
        down = lax.ppermute(have[1], "col", [(s, (s - step) % ncol) for s in sources])
        have = jnp.where(lax.rem(col_id, 2 * step) < 2, have, jnp.stack([up, down]))
    up = lax.ppermute(have[0], "col", [(s, (s + 1) % ncol) for s in range(ncol)])
    down = lax.ppermute(have[1], "col", [(s, (s - 1) % ncol) for s in range(ncol)])
    near = jnp.stack([up, down])
    even = lax.rem(col_id, 2) == 0
    return jnp.where(even, have, near), jnp.where(even, near, have)


def spread_columns(mine, row_id, nrow, ncol):
    width = mine.shape[-1]
    core = lax.rem(row_id, 2)
    quarter = width // 4
    part = 0.0
    for k in range(4):
        pairs = []
        for row in range(nrow):
            for column in (0, 1):
                target = row_of(k, column + 2 * (row // ncol), 0)
                pairs.append((row * ncol + column, target * ncol + row % ncol))
        part = part + lax.ppermute(mine[:, k * quarter:(k + 1) * quarter], ("row", "col"), pairs)
    swap = [(row, row ^ 1) for row in range(nrow)]
    piece = jnp.where(core == 0, part[0], lax.ppermute(part[1], "row", swap))
    groups = [list(range(c, nrow, 2)) for c in range(2)]
    own = jnp.broadcast_to(piece[None], (nrow // 2, quarter, width))
    own = lax.all_to_all(own, "row", 0, 0, axis_index_groups=groups).reshape(4, width, width)
    return own, lax.ppermute(own, "row", swap)


def on_device(matrix, structure):
    lbr = matrix.shape[0]
    lbc = matrix.shape[2]
    width = matrix.shape[4]
    blocks = matrix.reshape(lbr, lbc, width, width)
    nrow = lax.axis_size("row")
    ncol = lax.axis_size("col")
    row_id = lax.axis_index("row")
    col_id = lax.axis_index("col")
    mine = blocks[:, 0]

    raw = spread_diagonal(mine[0], col_id)
    own, other = spread_columns(mine, row_id, nrow, ncol)
    rows0, rows1 = spread_rows(mine, col_id, ncol)

    ids = jnp.stack([row_id, col_id, row_id // 2, lax.rem(row_id, 2)]).astype(jnp.int32)
    vmem = pl.BlockSpec(memory_space=pltpu.VMEM)
    smem = pl.BlockSpec(memory_space=pltpu.SMEM)
    params = pltpu.CompilerParams(vmem_limit_bytes=40 * 2**20)
    inv, low, high, rest = pl.pallas_call(
        head_kernel,
        out_shape=[
            jax.ShapeDtypeStruct((3, 2, width, width), jnp.bfloat16),
            jax.ShapeDtypeStruct((width, width), jnp.float32),
            jax.ShapeDtypeStruct((lbc, width, 2 * width), jnp.bfloat16),
            jax.ShapeDtypeStruct((lbc, width, 2 * width), jnp.bfloat16),
        ],
        in_specs=[smem] * 2 + [vmem] * 3,
        out_specs=[vmem] * 4,
        scratch_shapes=[pltpu.VMEM((width, width), jnp.float32)],
        compiler_params=params,
    )(ids, structure, raw, own, other)
    result = pl.pallas_call(
        tail_kernel,
        out_shape=jax.ShapeDtypeStruct(blocks.shape, jnp.float32),
        in_specs=[smem] * 2 + [vmem] * 7,
        out_specs=vmem,
        scratch_shapes=[pltpu.VMEM((width, 2 * width), jnp.bfloat16)] * 2,
        compiler_params=params,
    )(ids, structure, inv, low, high, rest, rows0, rows1, blocks)
    return result.reshape(matrix.shape)


def solution(mesh):
    in_specs = (P(None, "row", None, "col", None, None), P())
    out_specs = P(None, "row", None, "col", None, None)
    return jax.shard_map(
        on_device, mesh=mesh, in_specs=in_specs, out_specs=out_specs, check_vma=False
    )
```

```python
import jax
import jax.numpy as jnp
from jax import lax
from jax.experimental import pallas as pl
from jax.experimental.pallas import tpu as pltpu
from jax.sharding import PartitionSpec as P

ROWS = ((1,), (0,))
BOTH = ((1,), (1,))
NX, NY = 4, 4


def row_of(x, y, core):
    return (y % NY) * 2 * NX + (x % NX) * 2 + core


def parts(a):
    high = a.astype(jnp.bfloat16)
    return high, (a - high.astype(jnp.float32)).astype(jnp.bfloat16)


def mul_parts(a, b, dims):
    def one(x, y):
        return lax.dot_general(x, y, (dims, ((), ())), preferred_element_type=jnp.float32)

    return one(a[0], b[0]) + (one(a[0], b[1]) + one(a[1], b[0]))


def mul(a, b, dims):
    return mul_parts(parts(a), parts(b), dims)


def iotas(n):
    return lax.broadcasted_iota(jnp.int32, (n, n), 0), lax.broadcasted_iota(jnp.int32, (n, n), 1)


def inverse_factor(sym, inv):
    n = sym.shape[0]
    ri, ci = iotas(n)
    eye = jnp.where(ri == ci, 1.0, 0.0)
    half = jnp.where(ri > ci, 1.0, jnp.where(ri == ci, 0.5, 0.0))
    diag = jnp.where(ri == ci, sym, 0.0)
    scale_col = lax.rsqrt(jnp.sum(diag, axis=1, keepdims=True))
    scale_row = lax.rsqrt(jnp.sum(diag, axis=0, keepdims=True))
    unit = sym * scale_col * scale_row

    def residual(t):
        return mul(mul(t, unit, ROWS), t, BOTH) - eye

    def improve(carry):
        t, err, _, count = carry
        x = err * half
        t = mul((eye - x) + mul(x, x, ROWS), t, ROWS)
        err = residual(t)
        return t, err, jnp.sum(err * err), count + 1

    x = (unit - eye) * half
    t = (eye - x) + mul(x, x, ROWS)
    err = residual(t)
    start = (t, err, jnp.sum(err * err), jnp.int32(0))
    t, err, size, _ = lax.while_loop(lambda c: (c[2] > 1e-4) & (c[3] < 8), improve, start)
    x = err * half
    near = parts(x)
    x = x - mul_parts(near, near, BOTH) * half
    t = mul((eye - x) + mul_parts(near, near, ROWS), t, ROWS)
    inv[...] = t * scale_row

    @pl.when(jnp.logical_not(size <= 1e-4))
    def _():
        def pivot(k, carry):
            left, right = carry
            row_left = jnp.sum(jnp.where(ri == k, left, 0.0), axis=0, keepdims=True)
            row_right = jnp.sum(jnp.where(ri == k, right, 0.0), axis=0, keepdims=True)
            col = jnp.sum(jnp.where((ci == k) & (ri > k), left, 0.0), axis=1, keepdims=True)
            pick = lax.broadcasted_iota(jnp.int32, (1, n), 1) == k
            col = col / jnp.sum(jnp.where(pick, row_left, 0.0), axis=1, keepdims=True)
            return left - col * row_left, right - col * row_right

        left, right = lax.fori_loop(0, n, pivot, (sym, eye))
        pivots = jnp.sum(jnp.where(ri == ci, left, 0.0), axis=1, keepdims=True)
        inv[...] = right * lax.rsqrt(pivots)


def symmetric(block):
    ri, ci = iotas(block.shape[0])
    return jnp.where(ri >= ci, block, block.T)


def solve(a0, a1, keep0, keep1, inv0, p10, inv1):
    p0 = mul_parts(parts(a0), inv0, BOTH) * keep0
    rest = a1 - mul_parts(parts(p0), p10, BOTH)
    return p0, mul_parts(parts(rest), inv1, BOTH) * keep1


def head_kernel(ids, struct, raw, own, other, inv, low, high, rest, tmp):
    row, col, core = ids[0], ids[1], ids[2]
    n = raw.shape[-1]
    ri, ci = iotas(n)
    s0 = symmetric(raw[:, 0:8, :].reshape(n, n))
    inverse_factor(s0, tmp)
    t0 = tmp[...]
    inv0 = parts(t0)
    a10 = raw[:, 8:16, :].reshape(n, n)
    p10 = mul_parts(parts(a10), inv0, BOTH) * struct[0, 1].astype(jnp.float32)
    half10 = parts(p10)
    s1 = symmetric(raw[:, 16:24, :].reshape(n, n) - mul_parts(half10, half10, BOTH))
    inverse_factor(s1, tmp)
    inv1 = parts(tmp[...])
    for k, pair in enumerate((inv0, half10, inv1)):
        inv[k, 0] = pair[0]
        inv[k, 1] = pair[1]

    @pl.when((row == 0) & (col == 0))
    def _():
        low[...] = jnp.where(ri >= ci, mul_parts(parts(s0), inv0, BOTH), 0.0)

    @pl.when((row == 1) & (col == 1))
    def _():
        low[...] = jnp.where(ri >= ci, mul_parts(parts(s1), inv1, BOTH), 0.0)

    for q in range(4):
        mine = core == q // 2
        slot = 2 * (q % 2)
        a0 = jnp.where(mine, own[slot], other[slot])
        a1 = jnp.where(mine, own[slot + 1], other[slot + 1])
        glob = q * 16 + col
        keep0 = struct[0, glob].astype(jnp.float32)
        keep1 = struct[1, glob].astype(jnp.float32)
        both = solve(a0, a1, keep0, keep1, inv0, half10, inv1)
        for k in range(2):
            top, bottom = parts(both[k])
            high[q, :, k * n:(k + 1) * n] = top
            rest[q, :, k * n:(k + 1) * n] = bottom


def tail_kernel(ids, struct, inv, low, high, rest, have0, have1, near0, near1, mat, out, row_high, row_rest):
    row, col = ids[0], ids[1]
    even = lax.rem(col, 2) == 0
    n = mat.shape[-1]
    inv0, p10, inv1 = ((inv[k, 0], inv[k, 1]) for k in range(3))
    for p, (have, near) in enumerate(((have0, near0), (have1, near1))):
        i = p * 32 + row
        a0 = jnp.where(even, have[...], near[...])
        a1 = jnp.where(even, near[...], have[...])
        keep0 = struct[0, i].astype(jnp.float32)
        keep1 = struct[1, i].astype(jnp.float32)
        both = solve(a0, a1, keep0, keep1, inv0, p10, inv1)
        for k in range(2):
            top, bottom = parts(both[k])
            row_high[:, k * n:(k + 1) * n] = top
            row_rest[:, k * n:(k + 1) * n] = bottom
        for q in range(4):
            j = q * 16 + col

            @pl.when(i < j)
            def _():
                out[p, q] = mat[p, q]

            @pl.when(i >= j)
            def _():
                left = (row_high[...], row_rest[...])
                out[p, q] = mat[p, q] - mul_parts(left, (high[q], rest[q]), BOTH)

        @pl.when((col == 0) & (i > 0))
        def _():
            out[p, 0] = both[0]

        @pl.when((col == 1) & (i > 1))
        def _():
            out[p, 0] = both[1]

        if p == 0:
            @pl.when((col < 2) & (row == col))
            def _():
                out[p, 0] = low[...]


def after(a, *values):
    return lax.optimization_barrier((a,) + values)[0]


def on_device(matrix, structure):
    lbr = matrix.shape[0]
    lbc = matrix.shape[2]
    width = matrix.shape[4]
    blocks = matrix.reshape(lbr, lbc, width, width)
    nrow = lax.axis_size("row")
    ncol = lax.axis_size("col")
    row_id = lax.axis_index("row")
    col_id = lax.axis_index("col")
    quarter = width // 4
    swap = [(row, row ^ 1) for row in range(nrow)]
    mine = [blocks[p, 0] for p in range(lbr)]

    def scatter(block):
        return lax.all_to_all(block.reshape(nrow, width // nrow, width), "row", 0, 0)[0:2]

    diag = scatter(mine[0])
    both = jnp.stack([a for a in mine])
    part = 0.0
    for k in range(4):
        pairs = []
        for row in range(nrow):
            for column in (0, 1):
                target = row_of(k, column + 2 * (row // ncol), 0)
                pairs.append((row * ncol + column, target * ncol + row % ncol))
        part = part + lax.ppermute(both[:, k * quarter:(k + 1) * quarter], ("row", "col"), pairs)

    def spread(have, step):
        return [lax.ppermute(a, "col", sorted(((s + c) % ncol, (t + c) % ncol) for s, t in pairs for c in (0, 1)))
                for a, pairs in zip(have, (step, [(-s, -t) for s, t in step]))]

    def merged(have, near, step):
        def took(pairs):
            return sum((((col_id - t) % ncol) < 2) for _, t in pairs) > 0
        return [jnp.where(took(pairs), b, a) for a, b, pairs in zip(have, near, (step, [(-s, -t) for s, t in step]))]

    steps = [[(0, 6)], [(0, 2), (6, 10)], [(2, 4), (6, 8), (10, 12), (0, 14)]]
    far = spread([a for a in mine], steps[0])
    piece = jnp.where(lax.rem(row_id, 2) == 0, part[0], lax.ppermute(part[1], "row", swap))
    got = [lax.ppermute(diag, "col", [(s, s + d) for s in (0, 1)]) for d in (4, 12, 8)]
    diag = jnp.where(col_id < 2, diag, got[0] + got[1] + got[2])
    sources = [s for s in range(ncol) if s % 4 < 2]
    two_up = lax.ppermute(diag, "col", [(s, s + 2) for s in sources])
    mixed = lax.ppermute(diag, "col", [(s, (s - 1) % ncol if s % 4 == 0 else s + 1) for s in sources])
    one_up = lax.ppermute(diag, "col", [(s, s + 1) for s in sources if s % 4 == 0])
    one_down = lax.ppermute(diag[1], "col", [(s, s - 1) for s in sources if s % 4 == 1])
    place = lax.rem(col_id, 4)
    left = jnp.where(place == 0, diag, jnp.where(place == 1, one_up, jnp.where(place == 2, two_up, mixed)))
    right = jnp.where(place == 0, one_down, jnp.where(place == 1, diag[1], jnp.where(place == 2, mixed[1], two_up[1])))
    diag = jnp.concatenate([left[0], left[1], right])

    have = merged(mine, far, steps[0])
    near = spread(have, steps[1])
    have = merged(have, near, steps[1])
    last = spread(have, steps[2])
    have = merged(have, last, steps[2])
    rows = have + [lax.ppermute(a, "col", [(s, (s + d) % ncol) for s in range(ncol)]) for a, d in zip(have, (1, -1))]
    own = jnp.broadcast_to(piece[None], (nrow // 2,) + piece.shape)
    groups = [list(range(c, nrow, 2)) for c in range(2)]
    own = lax.all_to_all(own, "row", 0, 0, axis_index_groups=groups).reshape(4, width, width)
    other = lax.ppermute(own, "row", swap)
    raw = jnp.broadcast_to(diag[None], (nrow,) + diag.shape)
    raw = lax.all_to_all(raw, "row", 0, 0)
    own = own

    ids = jnp.stack([row_id, col_id, lax.rem(row_id, 2)]).astype(jnp.int32)
    vmem = pl.BlockSpec(memory_space=pltpu.VMEM)
    smem = pl.BlockSpec(memory_space=pltpu.SMEM)
    params = pltpu.CompilerParams(vmem_limit_bytes=40 * 2**20)
    inv, low, high, rest = pl.pallas_call(
        head_kernel,
        out_shape=[
            jax.ShapeDtypeStruct((3, 2, width, width), jnp.bfloat16),
            jax.ShapeDtypeStruct((width, width), jnp.float32),
            jax.ShapeDtypeStruct((lbc, width, 2 * width), jnp.bfloat16),
            jax.ShapeDtypeStruct((lbc, width, 2 * width), jnp.bfloat16),
        ],
        in_specs=[smem] * 2 + [vmem] * 3,
        out_specs=[vmem] * 4,
        scratch_shapes=[pltpu.VMEM((width, width), jnp.float32)],
        compiler_params=params,
        cost_estimate=pl.CostEstimate(flops=10000000000, bytes_accessed=2**22, transcendentals=0),
    )(ids, structure, raw, own, other)
    result = pl.pallas_call(
        tail_kernel,
        out_shape=jax.ShapeDtypeStruct(blocks.shape, jnp.float32),
        in_specs=[smem] * 2 + [vmem] * 9,
        out_specs=vmem,
        scratch_shapes=[pltpu.VMEM((width, 2 * width), jnp.bfloat16)] * 2,
        compiler_params=params,
        cost_estimate=pl.CostEstimate(flops=3 * 10**9, bytes_accessed=2**23, transcendentals=0),
    )(ids, structure, inv, low, high, rest, *rows, blocks)
    return result.reshape(matrix.shape)


def solution(mesh):
    in_specs = (P(None, "row", None, "col", None, None), P())
    out_specs = P(None, "row", None, "col", None, None)
    return jax.shard_map(
        on_device, mesh=mesh, in_specs=in_specs, out_specs=out_specs, check_vma=False
    )
```

```python
import jax
import jax.numpy as jnp
from jax import lax
from jax.experimental import pallas as pl
from jax.experimental.pallas import tpu as pltpu
from jax.sharding import PartitionSpec as P

ROWS = ((1,), (0,))
BOTH = ((1,), (1,))
NX, NY = 4, 4


def row_of(x, y, core):
    return (y % NY) * 2 * NX + (x % NX) * 2 + core


def parts(a):
    high = a.astype(jnp.bfloat16)
    return high, (a - high.astype(jnp.float32)).astype(jnp.bfloat16)


def mul_parts(a, b, dims):
    def one(x, y):
        return lax.dot_general(x, y, (dims, ((), ())), preferred_element_type=jnp.float32)

    return one(a[0], b[0]) + (one(a[0], b[1]) + one(a[1], b[0]))


def mul(a, b, dims):
    return mul_parts(parts(a), parts(b), dims)


def mul_rough(a, b, dims):
    a, b = a.astype(jnp.bfloat16), b.astype(jnp.bfloat16)
    return lax.dot_general(a, b, (dims, ((), ())), preferred_element_type=jnp.float32)


def iotas(n):
    return lax.broadcasted_iota(jnp.int32, (n, n), 0), lax.broadcasted_iota(jnp.int32, (n, n), 1)


def inverse_factor(sym, inv):
    n = sym.shape[0]
    ri, ci = iotas(n)
    eye = jnp.where(ri == ci, 1.0, 0.0)
    half = jnp.where(ri > ci, 1.0, jnp.where(ri == ci, 0.5, 0.0))
    diag = jnp.where(ri == ci, sym, 0.0)
    scale_col = lax.rsqrt(jnp.sum(diag, axis=1, keepdims=True))
    scale_row = lax.rsqrt(jnp.sum(diag, axis=0, keepdims=True))
    unit = sym * scale_col * scale_row

    def residual(t):
        return mul(mul(t, unit, ROWS), t, BOTH) - eye

    def improve(carry):
        t, err, _, count = carry
        x = err * half
        t = mul((eye - x) + mul_rough(x, x, ROWS), t, ROWS)
        err = residual(t)
        return t, err, jnp.sum(err * err), count + 1

    x = (unit - eye) * half
    t = (eye - x) + mul_rough(x, x, ROWS)
    err = residual(t)
    start = (t, err, jnp.sum(err * err), jnp.int32(0))
    t, err, size, _ = lax.while_loop(lambda c: (c[2] > 1e-4) & (c[3] < 8), improve, start)
    x = err * half
    twice = mul_rough(x, x, ROWS)
    x = x - mul_rough(x, x, BOTH) * half
    t = mul((eye - x) + twice, t, ROWS)
    inv[...] = t * scale_row

    @pl.when(jnp.logical_not(size <= 1e-4))
    def _():
        def pivot(k, carry):
            left, right = carry
            row_left = jnp.sum(jnp.where(ri == k, left, 0.0), axis=0, keepdims=True)
            row_right = jnp.sum(jnp.where(ri == k, right, 0.0), axis=0, keepdims=True)
            col = jnp.sum(jnp.where((ci == k) & (ri > k), left, 0.0), axis=1, keepdims=True)
            pick = lax.broadcasted_iota(jnp.int32, (1, n), 1) == k
            col = col / jnp.sum(jnp.where(pick, row_left, 0.0), axis=1, keepdims=True)
            return left - col * row_left, right - col * row_right

        left, right = lax.fori_loop(0, n, pivot, (sym, eye))
        pivots = jnp.sum(jnp.where(ri == ci, left, 0.0), axis=1, keepdims=True)
        inv[...] = right * lax.rsqrt(pivots)


def symmetric(block):
    ri, ci = iotas(block.shape[0])
    return jnp.where(ri >= ci, block, block.T)


def solve(a0, a1, keep0, keep1, inv0, p10, inv1):
    p0 = mul_parts(parts(a0), inv0, BOTH) * keep0
    rest = a1 - mul_parts(parts(p0), p10, BOTH)
    return p0, mul_parts(parts(rest), inv1, BOTH) * keep1


def head_kernel(ids, struct, raw, own, other, inv, low, high, rest, tmp):
    row, col, core = ids[0], ids[1], ids[2]
    n = raw.shape[-1]
    ri, ci = iotas(n)
    s0 = symmetric(raw[:, 0:8, :].reshape(n, n))
    inverse_factor(s0, tmp)
    t0 = tmp[...]
    inv0 = parts(t0)
    a10 = raw[:, 8:16, :].reshape(n, n)
    p10 = mul_parts(parts(a10), inv0, BOTH) * struct[0, 1].astype(jnp.float32)
    half10 = parts(p10)
    s1 = symmetric(raw[:, 16:24, :].reshape(n, n) - mul_parts(half10, half10, BOTH))
    inverse_factor(s1, tmp)
    inv1 = parts(tmp[...])
    for k, pair in enumerate((inv0, half10, inv1)):
        inv[k, 0] = pair[0]
        inv[k, 1] = pair[1]

    @pl.when((row == 0) & (col == 0))
    def _():
        low[...] = jnp.where(ri >= ci, mul_parts(parts(s0), inv0, BOTH), 0.0)

    @pl.when((row == 1) & (col == 1))
    def _():
        low[...] = jnp.where(ri >= ci, mul_parts(parts(s1), inv1, BOTH), 0.0)

    def block(q, k):
        slot = 2 * (q % 2) + k
        return jnp.where(core == q // 2, own[slot], other[slot])

    def keep(k):
        return jnp.concatenate([jnp.full((n, 1), struct[k, q * 16 + col].astype(jnp.float32)) for q in range(4)])

    def stack(k):
        return jnp.concatenate([block(q, k) for q in range(4)])

    both = solve(stack(0), stack(1), keep(0), keep(1), inv0, half10, inv1)
    for k in range(2):
        top, bottom = parts(both[k])
        high[:, :, k * n:(k + 1) * n] = top.reshape(4, n, n)
        rest[:, :, k * n:(k + 1) * n] = bottom.reshape(4, n, n)


def tail_kernel(ids, struct, inv, low, high, rest, have0, have1, near0, near1, mat, out, row_high, row_rest):
    row, col = ids[0], ids[1]
    even = lax.rem(col, 2) == 0
    n = mat.shape[-1]
    inv0, p10, inv1 = ((inv[k, 0], inv[k, 1]) for k in range(3))
    for p, (have, near) in enumerate(((have0, near0), (have1, near1))):
        i = p * 32 + row
        a0 = jnp.where(even, have[...], near[...])
        a1 = jnp.where(even, near[...], have[...])
        keep0 = struct[0, i].astype(jnp.float32)
        keep1 = struct[1, i].astype(jnp.float32)
        both = solve(a0, a1, keep0, keep1, inv0, p10, inv1)
        for k in range(2):
            top, bottom = parts(both[k])
            row_high[:, k * n:(k + 1) * n] = top
            row_rest[:, k * n:(k + 1) * n] = bottom
        for q in range(4):
            j = q * 16 + col

            @pl.when(i < j)
            def _():
                out[p, q] = mat[p, q]

            @pl.when(i >= j)
            def _():
                left = (row_high[...], row_rest[...])
                out[p, q] = mat[p, q] - mul_parts(left, (high[q], rest[q]), BOTH)

        @pl.when((col == 0) & (i > 0))
        def _():
            out[p, 0] = both[0]

        @pl.when((col == 1) & (i > 1))
        def _():
            out[p, 0] = both[1]

        if p == 0:
            @pl.when((col < 2) & (row == col))
            def _():
                out[p, 0] = low[...]


def after(a, *values):
    return lax.optimization_barrier((a,) + values)[0]


def on_device(matrix, structure):
    lbr = matrix.shape[0]
    lbc = matrix.shape[2]
    width = matrix.shape[4]
    blocks = matrix.reshape(lbr, lbc, width, width)
    nrow = lax.axis_size("row")
    ncol = lax.axis_size("col")
    row_id = lax.axis_index("row")
    col_id = lax.axis_index("col")
    quarter = width // 4
    swap = [(row, row ^ 1) for row in range(nrow)]
    mine = [blocks[p, 0] for p in range(lbr)]

    def scatter(block):
        return lax.all_to_all(block.reshape(nrow, width // nrow, width), "row", 0, 0)[0:2]

    diag = scatter(mine[0])

    def spread(have, step):
        return [lax.ppermute(a, "col", sorted(((s + c) % ncol, (t + c) % ncol) for s, t in pairs for c in (0, 1)))
                for a, pairs in zip(have, (step, [(-s, -t) for s, t in step]))]

    def merged(have, near, step):
        def took(pairs):
            return sum((((col_id - t) % ncol) < 2) for _, t in pairs) > 0
        return [jnp.where(took(pairs), b, a) for a, b, pairs in zip(have, near, (step, [(-s, -t) for s, t in step]))]

    steps = [[(0, 6)], [(0, 2), (6, 10)], [(2, 4), (6, 8), (10, 12), (0, 14)]]
    far = spread([a for a in mine], steps[0])
    have = merged(mine, far, steps[0])
    near = spread(have, steps[1])
    have = merged(have, near, steps[1])
    last = spread(have, steps[2])
    have = merged(have, last, steps[2])
    rows = have + [lax.ppermute(a, "col", [(s, (s + d) % ncol) for s in range(ncol)]) for a, d in zip(have, (1, -1))]
    both = jnp.stack([a for a in mine])
    part = 0.0
    for k in range(4):
        pairs = []
        for row in range(nrow):
            for column in (0, 1):
                target = row_of(k, column + 2 * (row // ncol), 0)
                pairs.append((row * ncol + column, target * ncol + row % ncol))
        part = part + lax.ppermute(both[:, k * quarter:(k + 1) * quarter], ("row", "col"), pairs)
    piece = jnp.where(lax.rem(row_id, 2) == 0, part[0], lax.ppermute(part[1], "row", swap))
    got = [lax.ppermute(diag, "col", [(s, s + d) for s in (0, 1)]) for d in (4, 12, 8)]
    diag = jnp.where(col_id < 2, diag, got[0] + got[1] + got[2])
    sources = [s for s in range(ncol) if s % 4 < 2]
    two_up = lax.ppermute(diag, "col", [(s, s + 2) for s in sources])
    mixed = lax.ppermute(diag, "col", [(s, (s - 1) % ncol if s % 4 == 0 else s + 1) for s in sources])
    one_up = lax.ppermute(diag, "col", [(s, s ^ 1) for s in range(ncol)])
    place = lax.rem(col_id, 4)
    left = jnp.where(place == 0, diag, jnp.where(place == 1, one_up, jnp.where(place == 2, two_up, mixed)))
    right = jnp.where(place == 0, one_up[1], jnp.where(place == 1, diag[1], jnp.where(place == 2, mixed[1], two_up[1])))
    diag = jnp.concatenate([left[0], left[1], right])

    own = jnp.broadcast_to(piece[None], (nrow // 2,) + piece.shape)
    groups = [list(range(c, nrow, 2)) for c in range(2)]
    own = lax.all_to_all(own, "row", 0, 0, axis_index_groups=groups).reshape(4, width, width)
    other = lax.ppermute(own, "row", swap)
    raw = jnp.broadcast_to(diag[None], (nrow,) + diag.shape)
    raw = lax.all_to_all(raw, "row", 0, 0)
    own = own

    ids = jnp.stack([row_id, col_id, lax.rem(row_id, 2)]).astype(jnp.int32)
    vmem = pl.BlockSpec(memory_space=pltpu.VMEM)
    smem = pl.BlockSpec(memory_space=pltpu.SMEM)
    params = pltpu.CompilerParams(vmem_limit_bytes=40 * 2**20)
    inv, low, high, rest = pl.pallas_call(
        head_kernel,
        out_shape=[
            jax.ShapeDtypeStruct((3, 2, width, width), jnp.bfloat16),
            jax.ShapeDtypeStruct((width, width), jnp.float32),
            jax.ShapeDtypeStruct((lbc, width, 2 * width), jnp.bfloat16),
            jax.ShapeDtypeStruct((lbc, width, 2 * width), jnp.bfloat16),
        ],
        in_specs=[smem] * 2 + [vmem] * 3,
        out_specs=[vmem] * 4,
        scratch_shapes=[pltpu.VMEM((width, width), jnp.float32)],
        compiler_params=params,
        cost_estimate=pl.CostEstimate(flops=10000000000, bytes_accessed=2**22, transcendentals=0),
    )(ids, structure, raw, own, other)
    result = pl.pallas_call(
        tail_kernel,
        out_shape=jax.ShapeDtypeStruct(blocks.shape, jnp.float32),
        in_specs=[smem] * 2 + [vmem] * 9,
        out_specs=vmem,
        scratch_shapes=[pltpu.VMEM((width, 2 * width), jnp.bfloat16)] * 2,
        compiler_params=params,
        cost_estimate=pl.CostEstimate(flops=3 * 10**9, bytes_accessed=2**23, transcendentals=0),
    )(ids, structure, inv, low, high, rest, *rows, blocks)
    return result.reshape(matrix.shape)


def solution(mesh):
    in_specs = (P(None, "row", None, "col", None, None), P())
    out_specs = P(None, "row", None, "col", None, None)
    return jax.shard_map(
        on_device, mesh=mesh, in_specs=in_specs, out_specs=out_specs, check_vma=False
    )
```

```python
import jax
import jax.numpy as jnp
from jax import lax
from jax.experimental import pallas as pl
from jax.experimental.pallas import tpu as pltpu
from jax.sharding import PartitionSpec as P

ROWS = ((1,), (0,))
BOTH = ((1,), (1,))
NX, NY = 4, 4


def row_of(x, y, core):
    return (y % NY) * 2 * NX + (x % NX) * 2 + core


def parts(a):
    high = a.astype(jnp.bfloat16)
    return high, (a - high.astype(jnp.float32)).astype(jnp.bfloat16)


def mul_parts(a, b, dims):
    def one(x, y):
        return lax.dot_general(x, y, (dims, ((), ())), preferred_element_type=jnp.float32)

    return one(a[0], b[0]) + (one(a[0], b[1]) + one(a[1], b[0]))


def mul(a, b, dims):
    return mul_parts(parts(a), parts(b), dims)


def mul_rough(a, b, dims):
    a, b = a.astype(jnp.bfloat16), b.astype(jnp.bfloat16)
    return lax.dot_general(a, b, (dims, ((), ())), preferred_element_type=jnp.float32)


def iotas(n):
    return lax.broadcasted_iota(jnp.int32, (n, n), 0), lax.broadcasted_iota(jnp.int32, (n, n), 1)


def inverse_factor(sym, inv):
    n = sym.shape[0]
    ri, ci = iotas(n)
    eye = jnp.where(ri == ci, 1.0, 0.0)
    half = jnp.where(ri > ci, 1.0, jnp.where(ri == ci, 0.5, 0.0))
    diag = jnp.where(ri == ci, sym, 0.0)
    scale_col = lax.rsqrt(jnp.sum(diag, axis=1, keepdims=True))
    scale_row = lax.rsqrt(jnp.sum(diag, axis=0, keepdims=True))
    unit = sym * scale_col * scale_row

    def residual(t):
        return mul(mul(t, unit, ROWS), t, BOTH) - eye

    def improve(carry):
        t, err, _, count = carry
        x = err * half
        t = mul((eye - x) + mul_rough(x, x, ROWS), t, ROWS)
        err = residual(t)
        return t, err, jnp.sum(err * err), count + 1

    x = (unit - eye) * half
    t = (eye - x) + mul_rough(x, x, ROWS)
    err = residual(t)
    start = (t, err, jnp.sum(err * err), jnp.int32(0))
    t, err, size, _ = lax.while_loop(lambda c: (c[2] > 1e-4) & (c[3] < 8), improve, start)
    x = err * half
    twice = mul_rough(x, x, ROWS)
    x = x - mul_rough(x, x, BOTH) * half
    t = mul((eye - x) + twice, t, ROWS)
    inv[...] = t * scale_row

    @pl.when(jnp.logical_not(size <= 1e-4))
    def _():
        def pivot(k, carry):
            left, right = carry
            row_left = jnp.sum(jnp.where(ri == k, left, 0.0), axis=0, keepdims=True)
            row_right = jnp.sum(jnp.where(ri == k, right, 0.0), axis=0, keepdims=True)
            col = jnp.sum(jnp.where((ci == k) & (ri > k), left, 0.0), axis=1, keepdims=True)
            pick = lax.broadcasted_iota(jnp.int32, (1, n), 1) == k
            col = col / jnp.sum(jnp.where(pick, row_left, 0.0), axis=1, keepdims=True)
            return left - col * row_left, right - col * row_right

        left, right = lax.fori_loop(0, n, pivot, (sym, eye))
        pivots = jnp.sum(jnp.where(ri == ci, left, 0.0), axis=1, keepdims=True)
        inv[...] = right * lax.rsqrt(pivots)


def symmetric(block):
    ri, ci = iotas(block.shape[0])
    return jnp.where(ri >= ci, block, block.T)


def solve(a0, a1, keep0, keep1, inv0, p10, inv1):
    p0 = mul_parts(parts(a0), inv0, BOTH) * keep0
    rest = a1 - mul_parts(parts(p0), p10, BOTH)
    return p0, mul_parts(parts(rest), inv1, BOTH) * keep1


def head_kernel(ids, struct, raw, own, other, inv, low, high, rest, tmp):
    row, col, core = ids[0], ids[1], ids[2]
    n = raw.shape[-1]
    ri, ci = iotas(n)
    s0 = symmetric(raw[:, 0:8, :].reshape(n, n))
    inverse_factor(s0, tmp)
    t0 = tmp[...]
    inv0 = parts(t0)
    a10 = raw[:, 8:16, :].reshape(n, n)
    p10 = mul_parts(parts(a10), inv0, BOTH) * struct[0, 1].astype(jnp.float32)
    half10 = parts(p10)
    s1 = symmetric(raw[:, 16:24, :].reshape(n, n) - mul_parts(half10, half10, BOTH))
    inverse_factor(s1, tmp)
    inv1 = parts(tmp[...])
    for k, pair in enumerate((inv0, half10, inv1)):
        inv[k, 0] = pair[0]
        inv[k, 1] = pair[1]

    @pl.when((row == 0) & (col == 0))
    def _():
        low[...] = jnp.where(ri >= ci, mul_parts(parts(s0), inv0, BOTH), 0.0)

    @pl.when((row == 1) & (col == 1))
    def _():
        low[...] = jnp.where(ri >= ci, mul_parts(parts(s1), inv1, BOTH), 0.0)

    def block(q, k):
        slot = 2 * (q % 2) + k
        return jnp.where(core == q // 2, own[slot], other[slot])

    def keep(k):
        return jnp.concatenate([jnp.full((n, 1), struct[k, q * 16 + col].astype(jnp.float32)) for q in range(4)])

    def stack(k):
        return jnp.concatenate([block(q, k) for q in range(4)])

    both = solve(stack(0), stack(1), keep(0), keep(1), inv0, half10, inv1)
    for k in range(2):
        top, bottom = parts(both[k])
        high[:, :, k * n:(k + 1) * n] = top.reshape(4, n, n)
        rest[:, :, k * n:(k + 1) * n] = bottom.reshape(4, n, n)


def tail_kernel(ids, struct, inv, low, high, rest, have0, have1, near0, near1, mat, out, row_high, row_rest, held, came, left):
    row, col = ids[0], ids[1]
    even = lax.rem(col, 2) == 0
    n = mat.shape[-1]
    spots = [(p, q) for p in range(2) for q in range(4)]
    reads = {s: pltpu.make_async_copy(mat.at[s], held.at[s], came.at[s]) for s in spots}
    writes = {s: pltpu.make_async_copy(held.at[s], out.at[s], left.at[s]) for s in spots}
    for s in spots:
        reads[s].start()
    inv0, p10, inv1 = ((inv[k, 0], inv[k, 1]) for k in range(3))
    have = jnp.concatenate([have0[...], have1[...]])
    near = jnp.concatenate([near0[...], near1[...]])

    def keep(k):
        return jnp.concatenate([jnp.full((n, 1), struct[k, p * 32 + row].astype(jnp.float32)) for p in range(2)])

    both = solve(jnp.where(even, have, near), jnp.where(even, near, have), keep(0), keep(1), inv0, p10, inv1)
    for k in range(2):
        top, bottom = parts(both[k])
        row_high[:, k * n:(k + 1) * n] = top
        row_rest[:, k * n:(k + 1) * n] = bottom
    for p, q in spots:
        i = p * 32 + row
        j = q * 16 + col
        rows = slice(p * n, (p + 1) * n)
        reads[p, q].wait()

        @pl.when(i >= j)
        def _():
            held[p, q] = held[p, q] - mul_parts((row_high[rows], row_rest[rows]), (high[q], rest[q]), BOTH)

        if q == 0:
            @pl.when((col == 0) & (i > 0))
            def _():
                held[p, 0] = both[0][rows]

            @pl.when((col == 1) & (i > 1))
            def _():
                held[p, 0] = both[1][rows]

        if p == 0 and q == 0:
            @pl.when((col < 2) & (row == col))
            def _():
                held[0, 0] = low[...]

        writes[p, q].start()
    for s in spots:
        writes[s].wait()


def after(a, *values):
    return lax.optimization_barrier((a,) + values)[0]


def on_device(matrix, structure):
    lbr = matrix.shape[0]
    lbc = matrix.shape[2]
    width = matrix.shape[4]
    blocks = matrix.reshape(lbr, lbc, width, width)
    nrow = lax.axis_size("row")
    ncol = lax.axis_size("col")
    row_id = lax.axis_index("row")
    col_id = lax.axis_index("col")
    quarter = width // 4
    swap = [(row, row ^ 1) for row in range(nrow)]
    mine = [blocks[p, 0] for p in range(lbr)]

    def scatter(block):
        return lax.all_to_all(block.reshape(nrow, width // nrow, width), "row", 0, 0)[0:2]

    diag = scatter(mine[0])

    def spread(have, step):
        return [lax.ppermute(a, "col", sorted(((s + c) % ncol, (t + c) % ncol) for s, t in pairs for c in (0, 1)))
                for a, pairs in zip(have, (step, [(-s, -t) for s, t in step]))]

    def merged(have, near, step):
        def took(pairs):
            return sum((((col_id - t) % ncol) < 2) for _, t in pairs) > 0
        return [jnp.where(took(pairs), b, a) for a, b, pairs in zip(have, near, (step, [(-s, -t) for s, t in step]))]

    steps = [[(0, 6)], [(0, 2), (6, 10)], [(2, 4), (6, 8), (10, 12), (0, 14)]]
    far = spread([a for a in mine], steps[0])
    have = merged(mine, far, steps[0])
    near = spread(have, steps[1])
    have = merged(have, near, steps[1])
    last = spread(have, steps[2])
    have = merged(have, last, steps[2])
    rows = have + [lax.ppermute(a, "col", [(s, (s + d) % ncol) for s in range(ncol)]) for a, d in zip(have, (1, -1))]
    both = jnp.stack([a for a in mine])
    part = 0.0
    for k in range(4):
        pairs = []
        for row in range(nrow):
            for column in (0, 1):
                target = row_of(k, column + 2 * (row // ncol), 0)
                pairs.append((row * ncol + column, target * ncol + row % ncol))
        part = part + lax.ppermute(both[:, k * quarter:(k + 1) * quarter], ("row", "col"), pairs)
    piece = jnp.where(lax.rem(row_id, 2) == 0, part[0], lax.ppermute(part[1], "row", swap))
    got = [lax.ppermute(diag, "col", [(s, s + d) for s in (0, 1)]) for d in (4, 12, 8)]
    diag = jnp.where(col_id < 2, diag, got[0] + got[1] + got[2])
    sources = [s for s in range(ncol) if s % 4 < 2]
    two_up = lax.ppermute(diag, "col", [(s, s + 2) for s in sources])
    mixed = lax.ppermute(diag, "col", [(s, (s - 1) % ncol if s % 4 == 0 else s + 1) for s in sources])
    one_up = lax.ppermute(diag, "col", [(s, s ^ 1) for s in range(ncol)])
    place = lax.rem(col_id, 4)
    left = jnp.where(place == 0, diag, jnp.where(place == 1, one_up, jnp.where(place == 2, two_up, mixed)))
    right = jnp.where(place == 0, one_up[1], jnp.where(place == 1, diag[1], jnp.where(place == 2, mixed[1], two_up[1])))
    diag = jnp.concatenate([left[0], left[1], right])

    own = jnp.broadcast_to(piece[None], (nrow // 2,) + piece.shape)
    groups = [list(range(c, nrow, 2)) for c in range(2)]
    own = lax.all_to_all(own, "row", 0, 0, axis_index_groups=groups).reshape(4, width, width)
    other = lax.ppermute(own, "row", swap)
    raw = jnp.broadcast_to(diag[None], (nrow,) + diag.shape)
    raw = lax.all_to_all(raw, "row", 0, 0)
    own = own

    ids = jnp.stack([row_id, col_id, lax.rem(row_id, 2)]).astype(jnp.int32)
    vmem = pl.BlockSpec(memory_space=pltpu.VMEM)
    smem = pl.BlockSpec(memory_space=pltpu.SMEM)
    params = pltpu.CompilerParams(vmem_limit_bytes=40 * 2**20)
    inv, low, high, rest = pl.pallas_call(
        head_kernel,
        out_shape=[
            jax.ShapeDtypeStruct((3, 2, width, width), jnp.bfloat16),
            jax.ShapeDtypeStruct((width, width), jnp.float32),
            jax.ShapeDtypeStruct((lbc, width, 2 * width), jnp.bfloat16),
            jax.ShapeDtypeStruct((lbc, width, 2 * width), jnp.bfloat16),
        ],
        in_specs=[smem] * 2 + [vmem] * 3,
        out_specs=[vmem] * 4,
        scratch_shapes=[pltpu.VMEM((width, width), jnp.float32)],
        compiler_params=params,
        cost_estimate=pl.CostEstimate(flops=10000000000, bytes_accessed=2**22, transcendentals=0),
    )(ids, structure, raw, own, other)
    result = pl.pallas_call(
        tail_kernel,
        out_shape=jax.ShapeDtypeStruct(blocks.shape, jnp.float32),
        in_specs=[smem] * 2 + [vmem] * 8 + [pl.BlockSpec(memory_space=pl.ANY)],
        out_specs=pl.BlockSpec(memory_space=pl.ANY),
        scratch_shapes=[pltpu.VMEM((lbr * width, 2 * width), jnp.bfloat16)] * 2
        + [pltpu.VMEM(blocks.shape, jnp.float32)]
        + [pltpu.SemaphoreType.DMA((lbr, lbc))] * 2,
        compiler_params=params,
        cost_estimate=pl.CostEstimate(flops=3 * 10**9, bytes_accessed=2**23, transcendentals=0),
    )(ids, structure, inv, low, high, rest, *rows, blocks)
    return result.reshape(matrix.shape)


def solution(mesh):
    in_specs = (P(None, "row", None, "col", None, None), P())
    out_specs = P(None, "row", None, "col", None, None)
    return jax.shard_map(
        on_device, mesh=mesh, in_specs=in_specs, out_specs=out_specs, check_vma=False
    )
```
